32 devices in a mesh: groups: 2 (over y), layer: 8 (over z, x), feat: 2 (over core).
Axes of the slice: x: 2, y: 2, z: 4, core: 2. Of those that a mesh axis runs over, the one named last changes fastest.
Arguments:
- codes_idx: int32 [64, 1, 64], P(('groups', 'layer', 'feat')), parts along dimension 0, may hold values from 0 to 16383, as said below
- codes_val: bfloat16 [64, 1, 64], P(('groups', 'layer', 'feat')), parts along dimension 0, may hold values from 0.19921875 to 4
- decoder: bfloat16 [16384, 2304], P(('layer', 'feat')), may hold values from -0.75 to 0.75
- bias: float32 [2304], replicated, may hold values from -3 to 3
- target: bfloat16 [64, 2304], P(('groups', 'layer', 'feat')), parts along dimension 0, may hold values from -6 to 6
Outputs:
- recon: float32 [64, 2304], P(('groups', 'layer', 'feat')), parts along dimension 0
- grad_decoder: bfloat16 [32768, 2304], P(('groups', 'layer', 'feat')), parts along dimension 0
- gradient_active_codes: float32 [64, 1, 64], P(('groups', 'layer', 'feat')), parts along dimension 0
The draws below stay inside these ranges and needn't reach their ends.
There are 2 independent parts, one for each index of `groups`. The reference program is written for one: setup_inputs(seed, part) draws one part's arguments, and reference() takes and returns one part's arrays. A program takes and returns all parts, laid end to end along the dimension named above; an argument that names none is the same for every part. Nothing has to cross between parts.
Inputs may be any that keep to these rules, and one draw needn't show every extreme that they name: `codes_idx`: for each token and source layer, 64 different features of that layer's 16384, at most 16 of them in any aligned block of 1024 features, and exactly 16 in at least one such block; some 128-feature blocks are chosen far more often than others.
All inputs are finite; a program needn't handle non-finite values.
Results may differ from the reference program's by a relative error of at most 0.0048.
Values may be sent and summed in bfloat16 or wider, within the bound.
A program may use at most 64 MiB of HBM per device.

```python
import math
import jax
import jax.numpy as jnp
from jax import lax

D = 2304
FEATURE_WIDTH = 16384
K = 64
SPAN = 16
CAP = 16
B = 32
S = 1
G = 16384


def draw_codes_idx(key, part):
    key = jax.random.fold_in(key, 11)
    first, second, third = jax.random.split(key, 3)
    block_rows = FEATURE_WIDTH // SPAN
    random_jitter = jax.random.randint(first, (B, S, FEATURE_WIDTH), 0, 32768)
    preference_boost = jax.random.randint(second, (S, FEATURE_WIDTH // 128), 0, 4)
    extra_reward = jnp.repeat(preference_boost, 128, axis=1) * 16384
    ranking_score = (random_jitter + extra_reward[None, :, :]) * FEATURE_WIDTH + jnp.arange(FEATURE_WIDTH, dtype=jnp.int32)
    ranking_score = ranking_score.reshape(B, S, SPAN, block_rows)
    values, inside = lax.top_k(ranking_score, CAP)
    favoured = jax.random.randint(third, (B, S), 0, SPAN)
    blocks = jnp.arange(SPAN, dtype=jnp.int32)
    chosen_block = (blocks[None, None, :] == favoured[:, :, None])[..., None]
    ranked = jnp.where(chosen_block, values, values - 1400000000)
    feature_vectors = inside + (blocks * block_rows)[None, None, :, None]
    ranked = ranked.reshape(B, S, SPAN * CAP)
    feature_vectors = feature_vectors.reshape(B, S, SPAN * CAP)
    picked_values, picked = lax.top_k(ranked, K)
    return jnp.take_along_axis(feature_vectors, picked, axis=2).astype(jnp.int32)


def levels(stream_key, dims, cuts, least, top_value):
    factor_of, own = 1.0, jax.random.fold_in(stream_key, 6)
    for dim, shards_of in cuts:
        draws = jnp.exp(jax.random.uniform(jax.random.fold_in(own, dim), (shards_of,), jnp.float32, least / len(cuts), top_value / len(cuts)))
        factor_of = factor_of * jnp.repeat(draws, dims[dim] // shards_of).reshape([-1 if axis == dim else 1 for axis in range(len(dims))])
    return factor_of


def scatter_about(own_key, dims, spread, limit, shards=(), kind=jnp.bfloat16):
    result = jax.random.normal(own_key, dims, jnp.float32) * spread
    if len(shards) > 0:
        result = levels(own_key, dims, shards, -0.22, 0.18) * result
    return jnp.clip(result, min=-limit, max=limit).astype(kind)


def setup_inputs(seed: int = 0, part: int = 0) -> dict:
    key_of = jax.random.split(jax.random.key(seed), 6)
    own_keys = jax.random.split(jax.random.fold_in(key_of[5], part), 6)
    return {
        "codes_idx": draw_codes_idx(jax.random.fold_in(jax.random.fold_in(key_of[5], part), 71), part),
        "codes_val": jnp.clip(jnp.exp(math.log(4.0) - 2.9996462 * jax.random.uniform(own_keys[1], (B, S, K), jnp.float32) ** levels(own_keys[1], (B, S, K), ((0, 16),), -0.2, 0.2)), 0.19921875, 4.0).astype(jnp.bfloat16),
        "decoder": scatter_about(key_of[2], (G, D), (S * K) ** -0.5, 0.75, ((0, 16),)),
        "bias": scatter_about(key_of[3], (D,), 0.5, 3.0, (), jnp.float32),
        "target": scatter_about(own_keys[4], (B, D), 1.0, 6.0, ((0, 16),)),
    }


def reference(codes_idx, codes_val, decoder, bias, target):
    batch = codes_idx.shape[0]
    offsets = jnp.arange(S, dtype=jnp.int32)[None, :, None] * FEATURE_WIDTH
    columns = (offsets + codes_idx).reshape(batch, S * K).astype(jnp.int32)
    line = jnp.arange(batch, dtype=jnp.int32)[:, None]
    acts = jnp.zeros((batch, S * FEATURE_WIDTH), jnp.bfloat16).at[line, columns].set(codes_val.reshape(batch, S * K))
    recon = jnp.dot(acts, decoder, preferred_element_type=jnp.float32) + bias
    error = (recon - target.astype(jnp.float32)).astype(jnp.bfloat16)
    acts_layers = acts.reshape(batch, S, FEATURE_WIDTH).transpose(1, 0, 2)
    weight_layers = decoder.reshape(S, FEATURE_WIDTH, D)

    def per_layer(pair):
        block, weight = pair
        grad_w = lax.dot_general(block, error, (((0,), (0,)), ((), ())), preferred_element_type=jnp.float32)
        grad_a = lax.dot_general(error, weight, (((1,), (1,)), ((), ())), preferred_element_type=jnp.float32)
        return grad_w.astype(jnp.bfloat16), grad_a

    grad_w, grad_a = lax.map(per_layer, (acts_layers, weight_layers))
    grad_decoder = grad_w.reshape(S * FEATURE_WIDTH, D)
    grad_dense = grad_a.transpose(1, 0, 2).reshape(batch, S * FEATURE_WIDTH)
    gradient_active_codes = jnp.take_along_axis(grad_dense, columns, axis=1).reshape(batch, S, K)
    return recon, grad_decoder, gradient_active_codes
```

```python
import functools

import jax
import jax.numpy as jnp
from jax import lax
from jax.experimental import pallas as pl
from jax.experimental.pallas import tpu as pltpu
from jax.sharding import PartitionSpec as P

FEATURE_WIDTH = 16384
LANES = 128
MESH = pl.DeviceIdType.MESH
F32 = jnp.float32


def exchange_kernel(
    msg_ref, dec_hbm, bias_ref, target_ref,
    recon_ref, acts_ref, err_ref, grad_ref,
    dec, codes, wide, part, got, errs, gout, gin,
    dec_sem, send_sems, recv_sems,
):
    layers, feats = lax.axis_size("layer"), lax.axis_size("feat")
    n = layers * feats
    me = lax.axis_index("layer") * feats + lax.axis_index("feat")
    sources = msg_ref.shape[0]
    rows, width = dec.shape
    tokens = recon_ref.shape[0]
    blocks = rows // LANES
    span = n // sources
    base = lax.rem(me, span) * rows

    load = pltpu.make_async_copy(dec_hbm, dec, dec_sem)
    load.start()

    def place(t):
        return {"layer": t // feats, "feat": lax.rem(t, feats)}

    def others(body):
        def step(i, carry):
            body(lax.rem(me + i, n))
            return carry
        lax.fori_loop(1, n, step, 0)

    def send(src_of, dst, phase):
        def one(t):
            pltpu.make_async_remote_copy(
                src_ref=src_of(t), dst_ref=dst.at[me],
                send_sem=send_sems.at[phase], recv_sem=recv_sems.at[phase],
                device_id=place(t), device_id_type=MESH,
            ).start()
        others(one)

    def settle(buf, sem):
        view = buf.at[pl.ds(0, n - 1)]
        pltpu.make_async_copy(view, view, sem).wait()

    barrier = pltpu.get_barrier_semaphore()
    others(lambda t: pl.semaphore_signal(
        barrier, inc=1, device_id=place(t), device_id_type=MESH))
    pl.semaphore_wait(barrier, n - 1)

    send(lambda t: msg_ref.at[t // span], codes, 0)
    codes[me] = msg_ref[me // span]
    settle(codes, recv_sems.at[0])

    lane = lax.broadcasted_iota(jnp.int32, (1, LANES), 1)
    deep = lax.broadcasted_iota(jnp.int32, (LANES, LANES), 0)
    shelf = lax.broadcasted_iota(jnp.int32, (tokens * blocks, LANES), 0)
    k = LANES // tokens
    owner_ok = (shelf // blocks) == (lax.broadcasted_iota(jnp.int32, (tokens * blocks, LANES), 1) // k)
    block_of = lax.rem(shelf, blocks)

    def where_codes(d):
        pair = codes[d]
        local = pair[0:1].astype(jnp.int32) - base
        hi = jnp.right_shift(local, 7)
        lo = jnp.bitwise_and(local, LANES - 1)
        mine = owner_ok & (block_of == hi)
        onehot = jnp.where(deep == lo, 1.0, 0.0)
        return pair[1:2], mine, onehot

    def build(d, carry):
        val, mine, onehot = where_codes(d)
        a = jnp.where(mine, val, 0.0).astype(jnp.bfloat16)
        spread = lax.dot_general(
            a, onehot.astype(jnp.bfloat16), (((1,), (1,)), ((), ())), preferred_element_type=F32)
        wide[pl.ds(d * tokens, tokens)] = spread.reshape(tokens, blocks, LANES)
        return carry
    lax.fori_loop(0, n, build, 0, unroll=8)
    acts = jnp.concatenate(
        [wide[:, h, :].astype(jnp.bfloat16) for h in range(blocks)], axis=1)
    acts_ref[...] = acts

    load.wait()
    chunk = 768 if width % 768 == 0 else width
    for c in range(0, width, chunk):
        p = jnp.dot(acts, dec[:, c:c + chunk], preferred_element_type=F32)
        for d in range(n):
            part[d, :, c:c + chunk] = p[d * tokens:(d + 1) * tokens]
    send(lambda t: part.at[t], got, 1)
    got[me] = part[me]
    settle(got, recv_sems.at[1])

    total = got[0]
    for d in range(1, n):
        total += got[d]
    recon = total + bias_ref[...]
    recon_ref[...] = recon
    errs[me] = (recon - target_ref[...].astype(F32)).astype(jnp.bfloat16).astype(F32)
    send(lambda t: errs.at[me], errs, 2)
    settle(errs, recv_sems.at[2])

    err = jnp.concatenate([errs[d] for d in range(n)], axis=0).astype(jnp.bfloat16)
    err_ref[...] = err
    gd = lax.dot_general(err, dec[...], (((1,), (1,)), ((), ())), preferred_element_type=F32)
    for h in range(blocks):
        wide[:, h, :] = gd[:, h * LANES:(h + 1) * LANES]

    def pick(d, carry):
        _, mine, onehot = where_codes(d)
        g = wide[pl.ds(d * tokens, tokens)].reshape(tokens * blocks, LANES)
        taken = lax.dot_general(
            g, onehot, (((1,), (0,)), ((), ())), preferred_element_type=F32,
            precision=lax.Precision.HIGHEST)
        gout[d] = jnp.sum(jnp.where(mine, taken, 0.0), axis=0, keepdims=True)
        return carry
    lax.fori_loop(0, n, pick, 0, unroll=8)
    send(lambda t: gout.at[t], gin, 3)
    gin[me] = gout[me]
    settle(gin, recv_sems.at[3])
    for s in range(sources):
        grad_ref[s] = jnp.sum(gin[s * span:(s + 1) * span], axis=0)

    for phase, buf in ((0, codes), (1, got), (2, errs), (3, gin)):
        settle(buf, send_sems.at[phase])


def per_device(n, codes_idx, codes_val, decoder, bias, target):
    tokens, sources, active = codes_idx.shape
    rows, width = decoder.shape
    lanes = tokens * active
    msg = jnp.stack(
        [
            codes_idx.transpose(1, 0, 2).reshape(sources, lanes).astype(F32),
            codes_val.transpose(1, 0, 2).reshape(sources, lanes).astype(F32),
        ],
        axis=1,
    )
    everyone = n * tokens
    vmem = pl.BlockSpec(memory_space=pltpu.VMEM)
    recon, acts, err, grad = pl.pallas_call(
        exchange_kernel,
        out_shape=(
            jax.ShapeDtypeStruct((tokens, width), F32),
            jax.ShapeDtypeStruct((everyone, rows), jnp.bfloat16),
            jax.ShapeDtypeStruct((everyone, width), jnp.bfloat16),
            jax.ShapeDtypeStruct((sources, 1, lanes), F32),
        ),
        in_specs=[vmem, pl.BlockSpec(memory_space=pl.ANY), vmem, vmem],
        out_specs=(vmem, vmem, vmem, vmem),
        scratch_shapes=[
            pltpu.VMEM((rows, width), jnp.bfloat16),
            pltpu.VMEM((n, 2, lanes), F32),
            pltpu.VMEM((everyone, rows // LANES, LANES), F32),
            pltpu.VMEM((n, tokens, width), F32),
            pltpu.VMEM((n, tokens, width), F32),
            pltpu.VMEM((n, tokens, width), F32),
            pltpu.VMEM((n, 1, lanes), F32),
            pltpu.VMEM((n, 1, lanes), F32),
            pltpu.SemaphoreType.DMA,
            pltpu.SemaphoreType.DMA((4,)),
            pltpu.SemaphoreType.DMA((4,)),
        ],
        compiler_params=pltpu.CompilerParams(
            collective_id=0, has_side_effects=True, vmem_limit_bytes=40 * 1024 * 1024
        ),
    )(msg, decoder, bias.reshape(1, width), target)
    grad_w = lax.dot_general(
        acts, err, (((0,), (0,)), ((), ())), preferred_element_type=F32
    ).astype(jnp.bfloat16)
    gradient_active_codes = grad.reshape(sources, tokens, active).transpose(1, 0, 2)
    return recon, grad_w, gradient_active_codes


def solution(mesh):
    placed = (
        P(("groups", "layer", "feat"), None, None),
        P(("groups", "layer", "feat"), None, None),
        P(("layer", "feat"), None),
        P(),
        P(("groups", "layer", "feat"), None),
    )
    return jax.shard_map(
        functools.partial(per_device, mesh.shape["layer"] * mesh.shape["feat"]),
        mesh=mesh,
        in_specs=placed,
        out_specs=(
            P(("groups", "layer", "feat"), None),
            P(("groups", "layer", "feat"), None),
            P(("groups", "layer", "feat"), None, None),
        ),
        check_vma=False,
    )
```

```python
import functools

import jax
import jax.numpy as jnp
from jax import lax
from jax.experimental import pallas as pl
from jax.experimental.pallas import tpu as pltpu
from jax.sharding import PartitionSpec as P

FEATURE_WIDTH = 16384
LANES = 128
MESH = pl.DeviceIdType.MESH
F32 = jnp.float32


def exchange_kernel(
    idx_ref, val_ref, dec_hbm, bias_hbm, target_hbm,
    recon_ref, acts_ref, err_ref, grad_ref,
    dec, bias, target, msg, codes, wide, part, got, errs, gout, gin,
    load_sems, send_sems, recv_sems,
):
    layers, feats = lax.axis_size("layer"), lax.axis_size("feat")
    n = layers * feats
    me = lax.axis_index("layer") * feats + lax.axis_index("feat")
    sources = msg.shape[0]
    rows, width = dec.shape
    tokens = recon_ref.shape[0]
    blocks = rows // LANES
    span = n // sources
    base = lax.rem(me, span) * rows

    loads = [
        pltpu.make_async_copy(src, dst, load_sems.at[i])
        for i, (src, dst) in enumerate(((dec_hbm, dec), (bias_hbm, bias), (target_hbm, target)))
    ]
    for load in loads:
        load.start()
    for s in range(sources):
        idx = [idx_ref[t, s:s + 1, :].astype(F32) for t in range(tokens)]
        val = val_ref[s].astype(F32)
        msg[s, 0:1] = jnp.concatenate(idx, axis=1)
        msg[s, 1:2] = jnp.concatenate([val[t:t + 1] for t in range(tokens)], axis=1)

    def place(t):
        return {"layer": t // feats, "feat": lax.rem(t, feats)}

    def others(body):
        def step(i, carry):
            body(lax.rem(me + i, n))
            return carry
        lax.fori_loop(1, n, step, 0)

    def send(src_of, dst, phase):
        def one(t):
            pltpu.make_async_remote_copy(
                src_ref=src_of(t), dst_ref=dst.at[me],
                send_sem=send_sems.at[phase], recv_sem=recv_sems.at[phase],
                device_id=place(t), device_id_type=MESH,
            ).start()
        others(one)

    def settle(buf, sem):
        view = buf.at[pl.ds(0, n - 1)]
        pltpu.make_async_copy(view, view, sem).wait()

    barrier = pltpu.get_barrier_semaphore()
    others(lambda t: pl.semaphore_signal(
        barrier, inc=1, device_id=place(t), device_id_type=MESH))
    pl.semaphore_wait(barrier, n - 1)

    send(lambda t: msg.at[t // span], codes, 0)
    codes[me] = msg[me // span]
    settle(codes, recv_sems.at[0])

    lane = lax.broadcasted_iota(jnp.int32, (1, LANES), 1)
    deep = lax.broadcasted_iota(jnp.int32, (LANES, LANES), 0)
    shelf = lax.broadcasted_iota(jnp.int32, (tokens * blocks, LANES), 0)
    k = LANES // tokens
    owner_ok = (shelf // blocks) == (lax.broadcasted_iota(jnp.int32, (tokens * blocks, LANES), 1) // k)
    block_of = lax.rem(shelf, blocks)

    def where_codes(d):
        pair = codes[d]
        local = pair[0:1].astype(jnp.int32) - base
        hi = jnp.right_shift(local, 7)
        lo = jnp.bitwise_and(local, LANES - 1)
        mine = owner_ok & (block_of == hi)
        onehot = jnp.where(deep == lo, 1.0, 0.0)
        return pair[1:2], mine, onehot

    def build(d, carry):
        val, mine, onehot = where_codes(d)
        a = jnp.where(mine, val, 0.0).astype(jnp.bfloat16)
        spread = lax.dot_general(
            a, onehot.astype(jnp.bfloat16), (((1,), (1,)), ((), ())), preferred_element_type=F32)
        wide[pl.ds(d * tokens, tokens)] = spread.reshape(tokens, blocks, LANES)
        return carry
    lax.fori_loop(0, n, build, 0, unroll=8)
    acts = jnp.concatenate(
        [wide[:, h, :].astype(jnp.bfloat16) for h in range(blocks)], axis=1)
    acts_ref[...] = acts

    loads[0].wait()
    chunk = 768 if width % 768 == 0 else width
    for c in range(0, width, chunk):
        p = jnp.dot(acts, dec[:, c:c + chunk], preferred_element_type=F32)
        for d in range(n):
            part[d, :, c:c + chunk] = p[d * tokens:(d + 1) * tokens]
    send(lambda t: part.at[t], got, 1)
    got[me] = part[me]
    settle(got, recv_sems.at[1])

    loads[1].wait()
    loads[2].wait()
    total = got[0]
    for d in range(1, n):
        total += got[d]
    recon = total + bias[...][None, :]
    recon_ref[...] = recon
    errs[me] = (recon - target[...].astype(F32)).astype(jnp.bfloat16).astype(F32)
    send(lambda t: errs.at[me], errs, 2)
    settle(errs, recv_sems.at[2])

    err = jnp.concatenate([errs[d] for d in range(n)], axis=0).astype(jnp.bfloat16)
    err_ref[...] = err
    gd = lax.dot_general(err, dec[...], (((1,), (1,)), ((), ())), preferred_element_type=F32)
    for h in range(blocks):
        wide[:, h, :] = gd[:, h * LANES:(h + 1) * LANES]

    def pick(d, carry):
        _, mine, onehot = where_codes(d)
        g = wide[pl.ds(d * tokens, tokens)].reshape(tokens * blocks, LANES)
        taken = lax.dot_general(
            g, onehot, (((1,), (0,)), ((), ())), preferred_element_type=F32,
            precision=lax.Precision.HIGHEST)
        gout[d] = jnp.sum(jnp.where(mine, taken, 0.0), axis=0, keepdims=True)
        return carry
    lax.fori_loop(0, n, pick, 0, unroll=8)
    send(lambda t: gout.at[t], gin, 3)
    gin[me] = gout[me]
    settle(gin, recv_sems.at[3])
    for s in range(sources):
        grad_ref[s] = jnp.sum(gin[s * span:(s + 1) * span], axis=0)

    for phase, buf in ((0, codes), (1, got), (2, errs), (3, gin)):
        settle(buf, send_sems.at[phase])


def finish_kernel(
    acts_ref, err_ref, recon_ref, grad_ref,
    recon_hbm, gw_hbm, codes_hbm,
    gw, codes, sems,
):
    rows = gw.shape[0]
    sources, _, lanes = grad_ref.shape
    tokens = codes.shape[0]
    active = lanes // tokens
    for s in range(sources):
        line = grad_ref[s]
        for t in range(tokens):
            codes[t, s:s + 1, :] = line[:, t * active:(t + 1) * active]
    copies = [
        pltpu.make_async_copy(recon_ref, recon_hbm, sems.at[0]),
        pltpu.make_async_copy(codes, codes_hbm, sems.at[1]),
    ]
    for copy in copies:
        copy.start()
    err = err_ref[...]
    step = 256
    for i, r in enumerate(range(0, rows, step)):
        gw[r:r + step] = lax.dot_general(
            acts_ref[:, r:r + step], err, (((0,), (0,)), ((), ())), preferred_element_type=F32
        ).astype(jnp.bfloat16)
        copy = pltpu.make_async_copy(
            gw.at[pl.ds(r, step)], gw_hbm.at[pl.ds(r, step)], sems.at[2 + i])
        copy.start()
        copies.append(copy)
    for copy in copies:
        copy.wait()


def per_device(n, codes_idx, codes_val, decoder, bias, target):
    tokens, sources, active = codes_idx.shape
    rows, width = decoder.shape
    lanes = tokens * active
    everyone = n * tokens
    vmem = pl.BlockSpec(memory_space=pltpu.VMEM)
    hbm = pl.BlockSpec(memory_space=pl.ANY)
    recon, acts, err, grad = pl.pallas_call(
        exchange_kernel,
        out_shape=(
            jax.ShapeDtypeStruct((tokens, width), F32),
            jax.ShapeDtypeStruct((everyone, rows), jnp.bfloat16),
            jax.ShapeDtypeStruct((everyone, width), jnp.bfloat16),
            jax.ShapeDtypeStruct((sources, 1, lanes), F32),
        ),
        in_specs=[vmem, vmem, hbm, hbm, hbm],
        out_specs=(vmem, vmem, vmem, vmem),
        scratch_shapes=[
            pltpu.VMEM((rows, width), jnp.bfloat16),
            pltpu.VMEM((width,), F32),
            pltpu.VMEM((tokens, width), jnp.bfloat16),
            pltpu.VMEM((sources, 2, lanes), F32),
            pltpu.VMEM((n, 2, lanes), F32),
            pltpu.VMEM((everyone, rows // LANES, LANES), F32),
            pltpu.VMEM((n, tokens, width), F32),
            pltpu.VMEM((n, tokens, width), F32),
            pltpu.VMEM((n, tokens, width), F32),
            pltpu.VMEM((n, 1, lanes), F32),
            pltpu.VMEM((n, 1, lanes), F32),
            pltpu.SemaphoreType.DMA((3,)),
            pltpu.SemaphoreType.DMA((4,)),
            pltpu.SemaphoreType.DMA((4,)),
        ],
        compiler_params=pltpu.CompilerParams(
            collective_id=0, has_side_effects=True, vmem_limit_bytes=56 * 1024 * 1024
        ),
    )(codes_idx, codes_val.transpose(1, 0, 2), decoder, bias, target)
    return pl.pallas_call(
        finish_kernel,
        out_shape=(
            jax.ShapeDtypeStruct((tokens, width), F32),
            jax.ShapeDtypeStruct((rows, width), jnp.bfloat16),
            jax.ShapeDtypeStruct((tokens, sources, active), F32),
        ),
        in_specs=[vmem, vmem, vmem, vmem],
        out_specs=(hbm, hbm, hbm),
        scratch_shapes=[
            pltpu.VMEM((rows, width), jnp.bfloat16),
            pltpu.VMEM((tokens, sources, active), F32),
            pltpu.SemaphoreType.DMA((2 + rows // 256,)),
        ],
        compiler_params=pltpu.CompilerParams(vmem_limit_bytes=56 * 1024 * 1024),
    )(acts, err, recon, grad)


def solution(mesh):
    placed = (
        P(("groups", "layer", "feat"), None, None),
        P(("groups", "layer", "feat"), None, None),
        P(("layer", "feat"), None),
        P(),
        P(("groups", "layer", "feat"), None),
    )
    return jax.shard_map(
        functools.partial(per_device, mesh.shape["layer"] * mesh.shape["feat"]),
        mesh=mesh,
        in_specs=placed,
        out_specs=(
            P(("groups", "layer", "feat"), None),
            P(("groups", "layer", "feat"), None),
            P(("groups", "layer", "feat"), None, None),
        ),
        check_vma=False,
    )
```

```python
import functools

import jax
import jax.numpy as jnp
from jax import lax
from jax.experimental import pallas as pl
from jax.experimental.pallas import tpu as pltpu
from jax.sharding import PartitionSpec as P

FEATURE_WIDTH = 16384
LANES = 128
WIRE = jnp.bfloat16
MESH = pl.DeviceIdType.MESH
F32 = jnp.float32


def exchange_kernel(
    idx_ref, val_ref, dec_hbm, bias_hbm, target_hbm,
    recon_ref, acts_ref, err_ref, grad_ref,
    dec, bias, target, msg, codes, wide, part, half, outgoing, incoming, errs, gout, gin,
    load_sems, send_sems, recv_sems,
):
    layers, feats = lax.axis_size("layer"), lax.axis_size("feat")
    my_layer, my_feat = lax.axis_index("layer"), lax.axis_index("feat")
    n = layers * feats
    me = my_feat * layers + my_layer
    partner = 1 - my_feat
    sources = msg.shape[0]
    rows, width = dec.shape
    tokens = recon_ref.shape[0]
    blocks = rows // LANES
    span = n // sources
    device = my_layer * feats + my_feat
    base = lax.rem(device, span) * rows
    chunks, chunk = part.shape[0], part.shape[-1]
    sent = []

    loads = [
        pltpu.make_async_copy(src, dst, load_sems.at[i])
        for i, (src, dst) in enumerate(((dec_hbm, dec), (bias_hbm, bias), (target_hbm, target)))
    ]
    for load in loads:
        load.start()
    for s in range(sources):
        idx = [idx_ref[t, s:s + 1, :].astype(F32) for t in range(tokens)]
        val = val_ref[s].astype(F32)
        msg[s, 0:1] = jnp.concatenate(idx, axis=1)
        msg[s, 1:2] = jnp.concatenate([val[t:t + 1] for t in range(tokens)], axis=1)

    def place(t):
        return {"layer": lax.rem(t, layers), "feat": t // layers}

    def source_of(t):
        return (lax.rem(t, layers) * feats + t // layers) // span

    def others(body):
        def step(i, carry):
            body(lax.rem(me + i, n))
            return carry
        lax.fori_loop(1, n, step, 0)

    def other_layers(body):
        def step(i, carry):
            body(lax.rem(my_layer + i, layers))
            return carry
        lax.fori_loop(1, layers, step, 0)

    def push(src, dst, phase, where):
        pltpu.make_async_remote_copy(
            src_ref=src, dst_ref=dst,
            send_sem=send_sems.at[phase], recv_sem=recv_sems.at[phase],
            device_id=where, device_id_type=MESH,
        ).start()

    def settle(view, sem):
        pltpu.make_async_copy(view, view, sem).wait()

    def arrive(view, phase):
        settle(view, recv_sems.at[phase])
        sent.append((view, phase))

    barrier = pltpu.get_barrier_semaphore()
    others(lambda t: pl.semaphore_signal(
        barrier, inc=1, device_id=place(t), device_id_type=MESH))
    pl.semaphore_wait(barrier, n - 1)

    others(lambda t: push(msg.at[source_of(t)], codes.at[me], 0, place(t)))
    codes[me] = msg[device // span]
    arrive(codes.at[pl.ds(0, n - 1)], 0)

    lane = lax.broadcasted_iota(jnp.int32, (tokens * blocks, LANES), 1)
    deep = lax.broadcasted_iota(jnp.int32, (LANES, LANES), 0)
    shelf = lax.broadcasted_iota(jnp.int32, (tokens * blocks, LANES), 0)
    owner_ok = (shelf // blocks) == (lane // (LANES // tokens))
    block_of = lax.rem(shelf, blocks)

    def where_codes(d):
        pair = codes[d]
        local = pair[0:1].astype(jnp.int32) - base
        hi = jnp.right_shift(local, 7)
        lo = jnp.bitwise_and(local, LANES - 1)
        mine = owner_ok & (block_of == hi)
        onehot = jnp.where(deep == lo, 1.0, 0.0).astype(jnp.bfloat16)
        return pair[1:2], mine, onehot

    def build(d, carry):
        val, mine, onehot = where_codes(d)
        a = jnp.where(mine, val, 0.0).astype(jnp.bfloat16)
        spread = lax.dot_general(
            a, onehot, (((1,), (1,)), ((), ())), preferred_element_type=F32)
        wide[pl.ds(d * tokens, tokens)] = spread.reshape(tokens, blocks, LANES)
        return carry
    lax.fori_loop(0, n, build, 0, unroll=8)
    acts = jnp.concatenate(
        [wide[:, h, :].astype(jnp.bfloat16) for h in range(blocks)], axis=1)
    acts_ref[...] = acts

    chip, cross, share, forward, back = (1, 1 + chunks, 1 + 2 * chunks, 1 + 3 * chunks, 1 + 4 * chunks)
    loads[0].wait()
    for c in range(chunks):
        p = jnp.dot(acts, dec[:, c * chunk:(c + 1) * chunk], preferred_element_type=F32)
        for d in range(n):
            part[c, d // layers, d % layers] = p[d * tokens:(d + 1) * tokens]
        push(part.at[c, partner], half.at[c], chip + c, {"feat": partner})
    for c in range(chunks):
        arrive(half.at[c], chip + c)
        outgoing[c] = (part[c, my_feat] + half[c]).astype(WIRE)
        other_layers(lambda l, c=c: push(
            outgoing.at[c, l], incoming.at[c, my_layer], cross + c, {"layer": l}))
        incoming[c, my_layer] = outgoing[c, my_layer]
    loads[1].wait()
    loads[2].wait()
    for c in range(chunks):
        cols = slice(c * chunk, (c + 1) * chunk)
        arrive(incoming.at[c, pl.ds(0, layers - 1)], cross + c)
        total = incoming[c, 0].astype(F32)
        for l in range(1, layers):
            total += incoming[c, l].astype(F32)
        recon = total + bias[cols][None, :]
        recon_ref[:, cols] = recon
        errs[c, my_feat, my_layer] = (recon - target[:, cols].astype(F32)).astype(jnp.bfloat16)
        mine_at = errs.at[c, my_feat, my_layer]
        other_layers(lambda l, c=c, ref=mine_at: push(ref, ref, share + c, {"layer": l}))
    for c in range(chunks):
        arrive(errs.at[c, my_feat, pl.ds(0, layers - 1)], share + c)
        push(errs.at[c, my_feat], errs.at[c, my_feat], forward + c, {"feat": partner})
    gd = jnp.zeros((n * tokens, rows), F32)
    for c in range(chunks):
        cols = slice(c * chunk, (c + 1) * chunk)
        arrive(errs.at[c, partner], forward + c)
        err = jnp.concatenate(
            [errs[c, d // layers, d % layers].astype(F32) for d in range(n)], axis=0
        ).astype(jnp.bfloat16)
        err_ref[:, cols] = err
        gd += lax.dot_general(
            err, dec[:, cols], (((1,), (1,)), ((), ())), preferred_element_type=F32)
    for h in range(blocks):
        wide[:, h, :] = gd[:, h * LANES:(h + 1) * LANES]

    def pick(d, carry):
        _, mine, onehot = where_codes(d)
        g = wide[pl.ds(d * tokens, tokens)].reshape(tokens * blocks, LANES)
        high = g.astype(jnp.bfloat16)
        rest = g - high.astype(F32)
        middle = rest.astype(jnp.bfloat16)
        low = (rest - middle.astype(F32)).astype(jnp.bfloat16)
        taken = jnp.dot(
            jnp.concatenate([high, middle, low], axis=0), onehot, preferred_element_type=F32)
        rest_of = tokens * blocks
        taken = taken[:rest_of] + taken[rest_of:2 * rest_of] + taken[2 * rest_of:]
        gout[d] = jnp.sum(jnp.where(mine, taken, 0.0), axis=0, keepdims=True)
        return carry
    lax.fori_loop(0, n, pick, 0, unroll=8)
    others(lambda t: push(gout.at[t], gin.at[me], back, place(t)))
    gin[me] = gout[me]
    arrive(gin.at[pl.ds(0, n - 1)], back)
    per = span // feats
    for s in range(sources):
        line = gin[s * per:(s + 1) * per]
        for f in range(1, feats):
            line += gin[f * layers + s * per:f * layers + (s + 1) * per]
        grad_ref[s] = jnp.sum(line, axis=0)

    for view, phase in sent:
        settle(view, send_sems.at[phase])


def finish_kernel(
    acts_ref, err_ref, recon_ref, grad_ref,
    recon_hbm, gw_hbm, codes_hbm,
    gw, codes, sems,
):
    rows = gw.shape[0]
    sources, _, lanes = grad_ref.shape
    tokens = codes.shape[0]
    active = lanes // tokens
    for s in range(sources):
        line = grad_ref[s]
        for t in range(tokens):
            codes[t, s:s + 1, :] = line[:, t * active:(t + 1) * active]
    copies = [
        pltpu.make_async_copy(recon_ref, recon_hbm, sems.at[0]),
        pltpu.make_async_copy(codes, codes_hbm, sems.at[1]),
    ]
    for copy in copies:
        copy.start()
    err = err_ref[...]
    step = 256
    for i, r in enumerate(range(0, rows, step)):
        gw[r:r + step] = lax.dot_general(
            acts_ref[:, r:r + step], err, (((0,), (0,)), ((), ())), preferred_element_type=F32
        ).astype(jnp.bfloat16)
        copy = pltpu.make_async_copy(
            gw.at[pl.ds(r, step)], gw_hbm.at[pl.ds(r, step)], sems.at[2 + i])
        copy.start()
        copies.append(copy)
    for copy in copies:
        copy.wait()


def per_device(layers, feats, codes_idx, codes_val, decoder, bias, target):
    tokens, sources, active = codes_idx.shape
    rows, width = decoder.shape
    lanes = tokens * active
    n = layers * feats
    everyone = n * tokens
    chunks = 3
    chunk = width // chunks
    vmem = pl.BlockSpec(memory_space=pltpu.VMEM)
    hbm = pl.BlockSpec(memory_space=pl.ANY)
    recon, acts, err, grad = pl.pallas_call(
        exchange_kernel,
        out_shape=(
            jax.ShapeDtypeStruct((tokens, width), F32),
            jax.ShapeDtypeStruct((everyone, rows), jnp.bfloat16),
            jax.ShapeDtypeStruct((everyone, width), jnp.bfloat16),
            jax.ShapeDtypeStruct((sources, 1, lanes), F32),
        ),
        in_specs=[vmem, vmem, hbm, hbm, hbm],
        out_specs=(vmem, vmem, vmem, vmem),
        scratch_shapes=[
            pltpu.VMEM((rows, width), jnp.bfloat16),
            pltpu.VMEM((width,), F32),
            pltpu.VMEM((tokens, width), jnp.bfloat16),
            pltpu.VMEM((sources, 2, lanes), F32),
            pltpu.VMEM((n, 2, lanes), F32),
            pltpu.VMEM((everyone, rows // LANES, LANES), F32),
            pltpu.VMEM((chunks, feats, layers, tokens, chunk), F32),
            pltpu.VMEM((chunks, layers, tokens, chunk), F32),
            pltpu.VMEM((chunks, layers, tokens, chunk), WIRE),
            pltpu.VMEM((chunks, layers, tokens, chunk), WIRE),
            pltpu.VMEM((chunks, feats, layers, tokens, chunk), jnp.bfloat16),
            pltpu.VMEM((n, 1, lanes), F32),
            pltpu.VMEM((n, 1, lanes), F32),
            pltpu.SemaphoreType.DMA((3,)),
            pltpu.SemaphoreType.DMA((2 + 4 * chunks,)),
            pltpu.SemaphoreType.DMA((2 + 4 * chunks,)),
        ],
        compiler_params=pltpu.CompilerParams(
            collective_id=0, has_side_effects=True, vmem_limit_bytes=56 * 1024 * 1024
        ),
    )(codes_idx, codes_val.transpose(1, 0, 2), decoder, bias, target)
    return pl.pallas_call(
        finish_kernel,
        out_shape=(
            jax.ShapeDtypeStruct((tokens, width), F32),
            jax.ShapeDtypeStruct((rows, width), jnp.bfloat16),
            jax.ShapeDtypeStruct((tokens, sources, active), F32),
        ),
        in_specs=[vmem, vmem, vmem, vmem],
        out_specs=(hbm, hbm, hbm),
        scratch_shapes=[
            pltpu.VMEM((rows, width), jnp.bfloat16),
            pltpu.VMEM((tokens, sources, active), F32),
            pltpu.SemaphoreType.DMA((2 + rows // 256,)),
        ],
        compiler_params=pltpu.CompilerParams(vmem_limit_bytes=56 * 1024 * 1024),
    )(acts, err, recon, grad)


def solution(mesh):
    placed = (
        P(("groups", "layer", "feat"), None, None),
        P(("groups", "layer", "feat"), None, None),
        P(("layer", "feat"), None),
        P(),
        P(("groups", "layer", "feat"), None),
    )
    return jax.shard_map(
        functools.partial(per_device, mesh.shape["layer"], mesh.shape["feat"]),
        mesh=mesh,
        in_specs=placed,
        out_specs=(
            P(("groups", "layer", "feat"), None),
            P(("groups", "layer", "feat"), None),
            P(("groups", "layer", "feat"), None, None),
        ),
        check_vma=False,
    )
```

```python
import functools

import jax
import jax.numpy as jnp
from jax import lax
from jax.experimental import pallas as pl
from jax.experimental.pallas import tpu as pltpu
from jax.sharding import PartitionSpec as P

FEATURE_WIDTH = 16384
LANES = 128
WIRE = jnp.bfloat16
MESH = pl.DeviceIdType.MESH
F32 = jnp.float32


def exchange_kernel(
    idx_ref, val_ref, dec_hbm, bias_hbm, target_hbm,
    recon_ref, acts_ref, err_ref, grad_ref,
    dec, bias, target, msg, codes, wide, outgoing, incoming, errs, gout, gin,
    load_sems, send_sems, recv_sems,
):
    layers, feats = lax.axis_size("layer"), lax.axis_size("feat")
    my_layer, my_feat = lax.axis_index("layer"), lax.axis_index("feat")
    n = layers * feats
    me = my_feat * layers + my_layer
    sources = msg.shape[0]
    rows, width = dec.shape
    tokens = recon_ref.shape[0]
    blocks = rows // LANES
    span = n // sources
    device = my_layer * feats + my_feat
    base = lax.rem(device, span) * rows
    chunks, chunk = errs.shape[0], errs.shape[-1]
    sent = []

    loads = [
        pltpu.make_async_copy(src, dst, load_sems.at[i])
        for i, (src, dst) in enumerate(((dec_hbm, dec), (bias_hbm, bias), (target_hbm, target)))
    ]
    for load in loads:
        load.start()
    for s in range(sources):
        idx = [idx_ref[t, s:s + 1, :].astype(F32) for t in range(tokens)]
        val = val_ref[s].astype(F32)
        msg[s, 0:1] = jnp.concatenate(idx, axis=1)
        msg[s, 1:2] = jnp.concatenate([val[t:t + 1] for t in range(tokens)], axis=1)

    def place(t):
        return {"layer": lax.rem(t, layers), "feat": t // layers}

    def source_of(t):
        return (lax.rem(t, layers) * feats + t // layers) // span

    def others(body):
        def step(i, carry):
            body(lax.rem(me + i, n))
            return carry
        lax.fori_loop(1, n, step, 0)

    def push(src, dst, phase, where):
        pltpu.make_async_remote_copy(
            src_ref=src, dst_ref=dst,
            send_sem=send_sems.at[phase], recv_sem=recv_sems.at[phase],
            device_id=where, device_id_type=MESH,
        ).start()

    def settle(view, sem):
        pltpu.make_async_copy(view, view, sem).wait()

    def arrive(view, phase):
        settle(view, recv_sems.at[phase])
        sent.append((view, phase))

    barrier = pltpu.get_barrier_semaphore()
    others(lambda t: pl.semaphore_signal(
        barrier, inc=1, device_id=place(t), device_id_type=MESH))
    pl.semaphore_wait(barrier, n - 1)

    others(lambda t: push(msg.at[source_of(t)], codes.at[me], 0, place(t)))
    codes[me] = msg[device // span]
    arrive(codes.at[pl.ds(0, n - 1)], 0)

    lane = lax.broadcasted_iota(jnp.int32, (tokens * blocks, LANES), 1)
    deep = lax.broadcasted_iota(jnp.int32, (LANES, LANES), 0)
    shelf = lax.broadcasted_iota(jnp.int32, (tokens * blocks, LANES), 0)
    owner_ok = (shelf // blocks) == (lane // (LANES // tokens))
    block_of = lax.rem(shelf, blocks)

    def where_codes(d):
        pair = codes[d]
        local = pair[0:1].astype(jnp.int32) - base
        hi = jnp.right_shift(local, 7)
        lo = jnp.bitwise_and(local, LANES - 1)
        mine = owner_ok & (block_of == hi)
        onehot = jnp.where(deep == lo, 1.0, 0.0).astype(jnp.bfloat16)
        return pair[1:2], mine, onehot

    def build(d, carry):
        val, mine, onehot = where_codes(d)
        a = jnp.where(mine, val, 0.0).astype(jnp.bfloat16)
        spread = lax.dot_general(
            a, onehot, (((1,), (1,)), ((), ())), preferred_element_type=F32)
        wide[pl.ds(d * tokens, tokens)] = spread.reshape(tokens, blocks, LANES)
        return carry
    lax.fori_loop(0, n, build, 0, unroll=8)
    acts = jnp.concatenate(
        [wide[:, h, :].astype(jnp.bfloat16) for h in range(blocks)], axis=1)
    acts_ref[...] = acts

    cross, share, back = 1, 1 + chunks, 1 + 2 * chunks
    loads[0].wait()
    for c in range(chunks):
        p = jnp.dot(acts, dec[:, c * chunk:(c + 1) * chunk], preferred_element_type=F32)
        for d in range(n):
            outgoing[c, d] = p[d * tokens:(d + 1) * tokens].astype(WIRE)
        others(lambda t, c=c: push(outgoing.at[c, t], incoming.at[c, me], cross + c, place(t)))
        incoming[c, me] = outgoing[c, me]
    loads[1].wait()
    loads[2].wait()
    for c in range(chunks):
        cols = slice(c * chunk, (c + 1) * chunk)
        arrive(incoming.at[c, pl.ds(0, n - 1)], cross + c)
        total = incoming[c, 0].astype(F32)
        for d in range(1, n):
            total += incoming[c, d].astype(F32)
        recon = total + bias[cols][None, :]
        recon_ref[:, cols] = recon
        errs[c, me] = (recon - target[:, cols].astype(F32)).astype(jnp.bfloat16)
        mine_at = errs.at[c, me]
        others(lambda t, c=c, ref=mine_at: push(ref, ref, share + c, place(t)))
    gd = jnp.zeros((n * tokens, rows), F32)
    for c in range(chunks):
        cols = slice(c * chunk, (c + 1) * chunk)
        arrive(errs.at[c, pl.ds(0, n - 1)], share + c)
        err = jnp.concatenate(
            [errs[c, d].astype(F32) for d in range(n)], axis=0
        ).astype(jnp.bfloat16)
        err_ref[:, cols] = err
        gd += lax.dot_general(
            err, dec[:, cols], (((1,), (1,)), ((), ())), preferred_element_type=F32)
    for h in range(blocks):
        wide[:, h, :] = gd[:, h * LANES:(h + 1) * LANES]

    def pick(d, carry):
        _, mine, onehot = where_codes(d)
        g = wide[pl.ds(d * tokens, tokens)].reshape(tokens * blocks, LANES)
        high = g.astype(jnp.bfloat16)
        rest = g - high.astype(F32)
        middle = rest.astype(jnp.bfloat16)
        low = (rest - middle.astype(F32)).astype(jnp.bfloat16)
        taken = jnp.dot(
            jnp.concatenate([high, middle, low], axis=0), onehot, preferred_element_type=F32)
        rest_of = tokens * blocks
        taken = taken[:rest_of] + taken[rest_of:2 * rest_of] + taken[2 * rest_of:]
        gout[d] = jnp.sum(jnp.where(mine, taken, 0.0), axis=0, keepdims=True)
        return carry
    lax.fori_loop(0, n, pick, 0, unroll=8)
    others(lambda t: push(gout.at[t], gin.at[me], back, place(t)))
    gin[me] = gout[me]
    arrive(gin.at[pl.ds(0, n - 1)], back)
    per = span // feats
    for s in range(sources):
        line = gin[s * per:(s + 1) * per]
        for f in range(1, feats):
            line += gin[f * layers + s * per:f * layers + (s + 1) * per]
        grad_ref[s] = jnp.sum(line, axis=0)

    for view, phase in sent:
        settle(view, send_sems.at[phase])


def finish_kernel(
    acts_ref, err_ref, recon_ref, grad_ref,
    recon_hbm, gw_hbm, codes_hbm,
    gw, codes, sems,
):
    rows = gw.shape[0]
    sources, _, lanes = grad_ref.shape
    tokens = codes.shape[0]
    active = lanes // tokens
    for s in range(sources):
        line = grad_ref[s]
        for t in range(tokens):
            codes[t, s:s + 1, :] = line[:, t * active:(t + 1) * active]
    copies = [
        pltpu.make_async_copy(recon_ref, recon_hbm, sems.at[0]),
        pltpu.make_async_copy(codes, codes_hbm, sems.at[1]),
    ]
    for copy in copies:
        copy.start()
    err = err_ref[...]
    step = 128
    for i, r in enumerate(range(0, rows, step)):
        gw[r:r + step] = lax.dot_general(
            acts_ref[:, r:r + step], err, (((0,), (0,)), ((), ())), preferred_element_type=F32
        ).astype(jnp.bfloat16)
        copy = pltpu.make_async_copy(
            gw.at[pl.ds(r, step)], gw_hbm.at[pl.ds(r, step)], sems.at[2 + i])
        copy.start()
        copies.append(copy)
    for copy in copies:
        copy.wait()


def per_device(layers, feats, codes_idx, codes_val, decoder, bias, target):
    tokens, sources, active = codes_idx.shape
    rows, width = decoder.shape
    lanes = tokens * active
    n = layers * feats
    everyone = n * tokens
    chunks = 3
    chunk = width // chunks
    vmem = pl.BlockSpec(memory_space=pltpu.VMEM)
    hbm = pl.BlockSpec(memory_space=pl.ANY)
    recon, acts, err, grad = pl.pallas_call(
        exchange_kernel,
        out_shape=(
            jax.ShapeDtypeStruct((tokens, width), F32),
            jax.ShapeDtypeStruct((everyone, rows), jnp.bfloat16),
            jax.ShapeDtypeStruct((everyone, width), jnp.bfloat16),
            jax.ShapeDtypeStruct((sources, 1, lanes), F32),
        ),
        in_specs=[vmem, vmem, hbm, hbm, hbm],
        out_specs=(vmem, vmem, vmem, vmem),
        scratch_shapes=[
            pltpu.VMEM((rows, width), jnp.bfloat16),
            pltpu.VMEM((width,), F32),
            pltpu.VMEM((tokens, width), jnp.bfloat16),
            pltpu.VMEM((sources, 2, lanes), F32),
            pltpu.VMEM((n, 2, lanes), F32),
            pltpu.VMEM((everyone, rows // LANES, LANES), F32),
            pltpu.VMEM((chunks, n, tokens, chunk), WIRE),
            pltpu.VMEM((chunks, n, tokens, chunk), WIRE),
            pltpu.VMEM((chunks, n, tokens, chunk), jnp.bfloat16),
            pltpu.VMEM((n, 1, lanes), F32),
            pltpu.VMEM((n, 1, lanes), F32),
            pltpu.SemaphoreType.DMA((3,)),
            pltpu.SemaphoreType.DMA((2 + 2 * chunks,)),
            pltpu.SemaphoreType.DMA((2 + 2 * chunks,)),
        ],
        compiler_params=pltpu.CompilerParams(
            collective_id=0, has_side_effects=True, vmem_limit_bytes=56 * 1024 * 1024
        ),
    )(codes_idx, codes_val.transpose(1, 0, 2), decoder, bias, target)
    return pl.pallas_call(
        finish_kernel,
        out_shape=(
            jax.ShapeDtypeStruct((tokens, width), F32),
            jax.ShapeDtypeStruct((rows, width), jnp.bfloat16),
            jax.ShapeDtypeStruct((tokens, sources, active), F32),
        ),
        in_specs=[vmem, vmem, vmem, vmem],
        out_specs=(hbm, hbm, hbm),
        scratch_shapes=[
            pltpu.VMEM((rows, width), jnp.bfloat16),
            pltpu.VMEM((tokens, sources, active), F32),
            pltpu.SemaphoreType.DMA((2 + rows // 128,)),
        ],
        compiler_params=pltpu.CompilerParams(vmem_limit_bytes=56 * 1024 * 1024),
    )(acts, err, recon, grad)


def solution(mesh):
    placed = (
        P(("groups", "layer", "feat"), None, None),
        P(("groups", "layer", "feat"), None, None),
        P(("layer", "feat"), None),
        P(),
        P(("groups", "layer", "feat"), None),
    )
    return jax.shard_map(
        functools.partial(per_device, mesh.shape["layer"], mesh.shape["feat"]),
        mesh=mesh,
        in_specs=placed,
        out_specs=(
            P(("groups", "layer", "feat"), None),
            P(("groups", "layer", "feat"), None),
            P(("groups", "layer", "feat"), None, None),
        ),
        check_vma=False,
    )
```

```python
import functools

import jax
import jax.numpy as jnp
from jax import lax
from jax.experimental import pallas as pl
from jax.experimental.pallas import tpu as pltpu
from jax.sharding import PartitionSpec as P

FEATURE_WIDTH = 16384
LANES = 128
WIRE = jnp.bfloat16
MESH = pl.DeviceIdType.MESH
F32 = jnp.float32


def exchange_kernel(
    idx_ref, val_ref, dec_hbm, bias_hbm, target_hbm,
    recon_ref, acts_ref, err_ref, grad_ref,
    dec, bias, target, msg, codes, wide, outgoing, incoming, errs, gout, gin,
    load_sems, send_sems, recv_sems,
):
    layers, feats = lax.axis_size("layer"), lax.axis_size("feat")
    my_layer, my_feat = lax.axis_index("layer"), lax.axis_index("feat")
    n = layers * feats
    me = my_feat * layers + my_layer
    sources = msg.shape[0]
    rows, width = dec.shape
    tokens = recon_ref.shape[0]
    blocks = rows // LANES
    span = n // sources
    device = my_layer * feats + my_feat
    base = lax.rem(device, span) * rows
    chunks, chunk = errs.shape[0], errs.shape[-1]
    sent = []

    loads = [
        pltpu.make_async_copy(src, dst, load_sems.at[i])
        for i, (src, dst) in enumerate(((dec_hbm, dec), (bias_hbm, bias), (target_hbm, target)))
    ]
    for load in loads:
        load.start()
    for s in range(sources):
        idx = [idx_ref[t, s:s + 1, :].astype(F32) for t in range(tokens)]
        val = val_ref[s].astype(F32)
        msg[s, 0:1] = jnp.concatenate(idx, axis=1)
        msg[s, 1:2] = jnp.concatenate([val[t:t + 1] for t in range(tokens)], axis=1)

    def place(t):
        return {"layer": lax.rem(t, layers), "feat": t // layers}

    def source_of(t):
        return (lax.rem(t, layers) * feats + t // layers) // span

    def others(body):
        def step(i, carry):
            body(lax.rem(me + i, n))
            return carry
        lax.fori_loop(1, n, step, 0)

    def push(src, dst, phase, where):
        pltpu.make_async_remote_copy(
            src_ref=src, dst_ref=dst,
            send_sem=send_sems.at[phase], recv_sem=recv_sems.at[phase],
            device_id=where, device_id_type=MESH,
        ).start()

    def settle(view, sem):
        pltpu.make_async_copy(view, view, sem).wait()

    def arrive(view, phase):
        settle(view, recv_sems.at[phase])
        sent.append((view, phase))

    barrier = pltpu.get_barrier_semaphore()
    others(lambda t: pl.semaphore_signal(
        barrier, inc=1, device_id=place(t), device_id_type=MESH))
    pl.semaphore_wait(barrier, n - 1)

    others(lambda t: push(msg.at[source_of(t)], codes.at[me], 0, place(t)))
    codes[me] = msg[device // span]
    arrive(codes.at[pl.ds(0, n - 1)], 0)

    lane = lax.broadcasted_iota(jnp.int32, (tokens * blocks, LANES), 1)
    deep = lax.broadcasted_iota(jnp.int32, (LANES, LANES), 0)
    shelf = lax.broadcasted_iota(jnp.int32, (tokens * blocks, LANES), 0)
    owner_ok = (shelf // blocks) == (lane // (LANES // tokens))
    block_of = lax.rem(shelf, blocks)

    def where_codes(d):
        pair = codes[d]
        local = pair[0:1].astype(jnp.int32) - base
        hi = jnp.right_shift(local, 7)
        lo = jnp.bitwise_and(local, LANES - 1)
        mine = owner_ok & (block_of == hi)
        onehot = jnp.where(deep == lo, 1.0, 0.0).astype(jnp.bfloat16)
        return pair[1:2], mine, onehot

    def build(d, carry):
        val, mine, onehot = where_codes(d)
        a = jnp.where(mine, val, 0.0).astype(jnp.bfloat16)
        spread = lax.dot_general(
            a, onehot, (((1,), (1,)), ((), ())), preferred_element_type=F32)
        wide[pl.ds(d * tokens, tokens)] = spread.reshape(tokens, blocks, LANES)
        return carry
    lax.fori_loop(0, n, build, 0, unroll=16)
    acts = jnp.concatenate(
        [wide[:, h, :].astype(jnp.bfloat16) for h in range(blocks)], axis=1)
    acts_ref[...] = acts

    cross, share, back = 1, 1 + chunks, 1 + 2 * chunks
    loads[0].wait()
    for c in range(chunks):
        p = jnp.dot(acts, dec[:, c * chunk:(c + 1) * chunk], preferred_element_type=F32)
        for d in range(n):
            outgoing[c, d] = p[d * tokens:(d + 1) * tokens].astype(WIRE)
        others(lambda t, c=c: push(outgoing.at[c, t], incoming.at[c, me], cross + c, place(t)))
        incoming[c, me] = outgoing[c, me]
    loads[1].wait()
    loads[2].wait()
    for c in range(chunks):
        cols = slice(c * chunk, (c + 1) * chunk)
        arrive(incoming.at[c, pl.ds(0, n - 1)], cross + c)
        total = incoming[c, 0].astype(F32)
        for d in range(1, n):
            total += incoming[c, d].astype(F32)
        recon = total + bias[cols][None, :]
        recon_ref[:, cols] = recon
        errs[c, me] = (recon - target[:, cols].astype(F32)).astype(jnp.bfloat16)
        mine_at = errs.at[c, me]
        others(lambda t, c=c, ref=mine_at: push(ref, ref, share + c, place(t)))
    gd = jnp.zeros((n * tokens, rows), F32)
    for c in range(chunks):
        cols = slice(c * chunk, (c + 1) * chunk)
        arrive(errs.at[c, pl.ds(0, n - 1)], share + c)
        err = jnp.concatenate(
            [errs[c, d].astype(F32) for d in range(n)], axis=0
        ).astype(jnp.bfloat16)
        err_ref[:, cols] = err
        gd += lax.dot_general(
            err, dec[:, cols], (((1,), (1,)), ((), ())), preferred_element_type=F32)
    for h in range(blocks):
        wide[:, h, :] = gd[:, h * LANES:(h + 1) * LANES]

    def pick(d, carry):
        _, mine, onehot = where_codes(d)
        g = wide[pl.ds(d * tokens, tokens)].reshape(tokens * blocks, LANES)
        high = g.astype(jnp.bfloat16)
        rest = g - high.astype(F32)
        middle = rest.astype(jnp.bfloat16)
        low = (rest - middle.astype(F32)).astype(jnp.bfloat16)
        taken = jnp.dot(
            jnp.concatenate([high, middle, low], axis=0), onehot, preferred_element_type=F32)
        rest_of = tokens * blocks
        taken = taken[:rest_of] + taken[rest_of:2 * rest_of] + taken[2 * rest_of:]
        gout[d] = jnp.sum(jnp.where(mine, taken, 0.0), axis=0, keepdims=True)
        return carry
    lax.fori_loop(0, n, pick, 0, unroll=16)
    others(lambda t: push(gout.at[t], gin.at[me], back, place(t)))
    gin[me] = gout[me]
    arrive(gin.at[pl.ds(0, n - 1)], back)
    per = span // feats
    for s in range(sources):
        line = gin[s * per:(s + 1) * per]
        for f in range(1, feats):
            line += gin[f * layers + s * per:f * layers + (s + 1) * per]
        grad_ref[s] = jnp.sum(line, axis=0)

    for view, phase in sent:
        settle(view, send_sems.at[phase])


def finish_kernel(
    acts_ref, err_ref, recon_ref, grad_ref,
    recon_hbm, gw_hbm, codes_hbm,
    gw, codes, sems,
):
    rows = gw.shape[0]
    sources, _, lanes = grad_ref.shape
    tokens = codes.shape[0]
    active = lanes // tokens
    for s in range(sources):
        line = grad_ref[s]
        for t in range(tokens):
            codes[t, s:s + 1, :] = line[:, t * active:(t + 1) * active]
    copies = [
        pltpu.make_async_copy(recon_ref, recon_hbm, sems.at[0]),
        pltpu.make_async_copy(codes, codes_hbm, sems.at[1]),
    ]
    for copy in copies:
        copy.start()
    err = err_ref[...]
    step = 128
    for i, r in enumerate(range(0, rows, step)):
        gw[r:r + step] = lax.dot_general(
            acts_ref[:, r:r + step], err, (((0,), (0,)), ((), ())), preferred_element_type=F32
        ).astype(jnp.bfloat16)
        copy = pltpu.make_async_copy(
            gw.at[pl.ds(r, step)], gw_hbm.at[pl.ds(r, step)], sems.at[2 + i])
        copy.start()
        copies.append(copy)
    for copy in copies:
        copy.wait()


def per_device(layers, feats, codes_idx, codes_val, decoder, bias, target):
    tokens, sources, active = codes_idx.shape
    rows, width = decoder.shape
    lanes = tokens * active
    n = layers * feats
    everyone = n * tokens
    chunks = 3
    chunk = width // chunks
    vmem = pl.BlockSpec(memory_space=pltpu.VMEM)
    hbm = pl.BlockSpec(memory_space=pl.ANY)
    recon, acts, err, grad = pl.pallas_call(
        exchange_kernel,
        out_shape=(
            jax.ShapeDtypeStruct((tokens, width), F32),
            jax.ShapeDtypeStruct((everyone, rows), jnp.bfloat16),
            jax.ShapeDtypeStruct((everyone, width), jnp.bfloat16),
            jax.ShapeDtypeStruct((sources, 1, lanes), F32),
        ),
        in_specs=[vmem, vmem, hbm, hbm, hbm],
        out_specs=(vmem, vmem, vmem, vmem),
        scratch_shapes=[
            pltpu.VMEM((rows, width), jnp.bfloat16),
            pltpu.VMEM((width,), F32),
            pltpu.VMEM((tokens, width), jnp.bfloat16),
            pltpu.VMEM((sources, 2, lanes), F32),
            pltpu.VMEM((n, 2, lanes), F32),
            pltpu.VMEM((everyone, rows // LANES, LANES), F32),
            pltpu.VMEM((chunks, n, tokens, chunk), WIRE),
            pltpu.VMEM((chunks, n, tokens, chunk), WIRE),
            pltpu.VMEM((chunks, n, tokens, chunk), jnp.bfloat16),
            pltpu.VMEM((n, 1, lanes), F32),
            pltpu.VMEM((n, 1, lanes), F32),
            pltpu.SemaphoreType.DMA((3,)),
            pltpu.SemaphoreType.DMA((2 + 2 * chunks,)),
            pltpu.SemaphoreType.DMA((2 + 2 * chunks,)),
        ],
        compiler_params=pltpu.CompilerParams(
            collective_id=0, has_side_effects=True, vmem_limit_bytes=56 * 1024 * 1024
        ),
    )(codes_idx, codes_val.transpose(1, 0, 2), decoder, bias, target)
    return pl.pallas_call(
        finish_kernel,
        out_shape=(
            jax.ShapeDtypeStruct((tokens, width), F32),
            jax.ShapeDtypeStruct((rows, width), jnp.bfloat16),
            jax.ShapeDtypeStruct((tokens, sources, active), F32),
        ),
        in_specs=[vmem, vmem, vmem, vmem],
        out_specs=(hbm, hbm, hbm),
        scratch_shapes=[
            pltpu.VMEM((rows, width), jnp.bfloat16),
            pltpu.VMEM((tokens, sources, active), F32),
            pltpu.SemaphoreType.DMA((2 + rows // 128,)),
        ],
        compiler_params=pltpu.CompilerParams(vmem_limit_bytes=56 * 1024 * 1024),
    )(acts, err, recon, grad)


def solution(mesh):
    placed = (
        P(("groups", "layer", "feat"), None, None),
        P(("groups", "layer", "feat"), None, None),
        P(("layer", "feat"), None),
        P(),
        P(("groups", "layer", "feat"), None),
    )
    return jax.shard_map(
        functools.partial(per_device, mesh.shape["layer"], mesh.shape["feat"]),
        mesh=mesh,
        in_specs=placed,
        out_specs=(
            P(("groups", "layer", "feat"), None),
            P(("groups", "layer", "feat"), None),
            P(("groups", "layer", "feat"), None, None),
        ),
        check_vma=False,
    )
```
